32 devices in a mesh: gx: 8 (over z, y), gy: 4 (over x, core).
Axes of the slice: x: 2, y: 2, z: 4, core: 2. Of those that a mesh axis runs over, the one named last changes fastest.
Arguments:
- object_field: float32 [2, 2048, 4096], P(None, 'gy', 'gx'), may hold values from -6 to 6
- probe: float32 [2, 256, 256], replicated, may hold values from -4 to 4
- frames: float32 [4, 8, 8, 3, 256, 256], P('gy', 'gx'), may hold values from 0.2 to 5
- positions: int32 [4, 8, 24, 2], P('gy', 'gx'), may hold values from -128 to 384
- helpers: int32 [4, 8, 24, 1], P('gy', 'gx'), may hold values from 0 to 7; in each aligned block of 24 rows (0 to 23, 24 to 47, ..., all dimensions but the last counted through in order) at most 3 rows name the same one
- task_counts: int32 [4, 8], P('gy', 'gx'), may hold values from 6 to 24, as said below
Outputs:
- updated_field: float32 [2, 2048, 4096], P(None, 'gy', 'gx')
The draws below stay inside these ranges and needn't reach their ends.
Inputs may be any that keep to these rules, and one draw needn't show every extreme that they name: `helpers`: among one tile's 24 task slots no helper column is named more than 3 times, and in some tiles one is named exactly 3 times. `task_counts`: some tile has all 24 tasks valid.
All inputs are finite; a program needn't handle non-finite values.
Results may differ from the reference program's by a relative error of at most 0.0003.
Values sent between devices are 32-bit elements; how exact they have to be, the bound alone decides.
A program may use at most 192 MiB of HBM per device.

```python
import math
import jax
import jax.numpy as jnp
import numpy as np
from jax import lax

TILE = 512
PATCH = 256
TASKS = 24
TROWS = 4
TCOLS = 8
SLOT = 3
NROWS = 2048
NCOLS = 4096


def draw_task_counts(key, part):
    first_key, second_key = jax.random.split(jax.random.fold_in(key, 71))
    counted = jax.random.randint(first_key, (TROWS * TCOLS,), TASKS // 4, TASKS + 1)
    chosen = jax.random.randint(second_key, (), 0, TROWS * TCOLS)
    filled = jnp.where(jnp.arange(TROWS * TCOLS) == chosen, TASKS, counted)
    return filled.reshape(TROWS, TCOLS).astype(jnp.int32)


def set_ends(drawn, stream_key, least, largest):
    dims = drawn.shape
    spot = [jax.random.randint(jax.random.fold_in(stream_key, axis), (), 0, dims[axis]) for axis in range(len(dims))]
    drawn = drawn.at[tuple(spot)].set(least)
    longest = dims.index(max(dims))
    spot[longest] = (spot[longest] + 1) % dims[longest]
    return drawn.at[tuple(spot)].set(largest)


def shard_levels(rng, extent, cuts, least, largest):
    def one(position, parts):
        draws = jax.random.uniform(jax.random.fold_in(jax.random.fold_in(rng, 6), position), (parts,), jnp.float32, least / len(cuts), largest / len(cuts))
        return jnp.repeat(jnp.exp(draws), extent[position] // parts).reshape((-1,) + (1,) * (len(extent) - position - 1))

    loudness = one(*cuts[0])
    for cut in cuts[1:]:
        loudness = loudness * one(*cut)
    return loudness


def shared_out(stream_key, own, number, rows, amount, top, bound, lean):
    ranking = jax.random.permutation(stream_key, amount)
    heavy_load, common = load_shares(amount, rows * top, bound, lean, True), load_shares(amount, rows * top, bound, lean, False)
    places = jnp.arange(amount)

    def named(tallies, offset_by):
        used = int((tallies > 0).sum())
        fixed = max(1, used // 4)
        passed = fixed + (places - fixed + offset_by * (used - fixed)) % max(1, amount - fixed)
        return jnp.zeros((amount,), jnp.int32).at[ranking[jnp.where(places < fixed, places, passed)]].set(jnp.asarray(tallies, jnp.int32))

    tallies = jnp.where(number % 4 == 0, named(heavy_load, number // 4), named(common, number - number // 4 - 1))
    mixed = jax.random.permutation(jax.random.fold_in(own, 3), amount)
    donor, receiver = mixed[0:amount // 2 * 2:2], mixed[1:amount // 2 * 2:2]
    slack = jnp.minimum(tallies[donor] - 1, bound - tallies[receiver]) // 2
    slack = jnp.where((donor == ranking[0]) | (receiver == ranking[0]) | (tallies[receiver] == 0), 0, jnp.maximum(slack, 0))
    passed = jax.random.randint(jax.random.fold_in(own, 4), (amount // 2,), 0, 1 << 20) % (slack + 1)
    tallies = tallies.at[donor].add(-passed).at[receiver].add(passed)
    labels = jnp.searchsorted(jnp.cumsum(tallies), jnp.arange(rows * top), side="right").astype(jnp.int32)
    grid = labels.reshape(top, rows).T
    grid = grid[jax.random.permutation(jax.random.fold_in(own, 1), rows)]
    offset_by = jax.random.randint(jax.random.fold_in(own, 2), (rows, 1), 0, top)
    return jnp.take_along_axis(grid, (jnp.arange(top)[None, :] + offset_by) % top, axis=1)


def load_shares(number_of, total, most, slope, full):
    weights = [(1 << 20) // math.isqrt(rank ** slope) + 1 for rank in range(1, number_of + 1)]
    largest = most if full else min(most, max(-(-total // number_of), total * weights[0] // sum(weights)))
    least = 1 if total - largest >= number_of - 1 else 0
    given, spare = [largest] + [least] * (number_of - 1), total - largest - least * (number_of - 1)
    while spare > 0:
        free = [i for i in range(1, number_of) if given[i] < largest] or [i for i in range(1, number_of) if given[i] < most]
        mass, left = sum([weights[i] for i in free]), spare
        for i in free:
            addition = min(most - given[i], max(1, left * weights[i] // mass), spare)
            given[i] = given[i] + addition
            spare = spare - addition
    return np.array(given)


def centred(own_key, extent, width, reach, cuts=(), kind=jnp.bfloat16):
    values = jax.random.normal(own_key, extent, jnp.float32) * width
    if len(cuts) > 0:
        values = shard_levels(own_key, extent, cuts, -0.22, 0.18) * values
    return jnp.clip(values, min=-reach, max=reach).astype(kind)


def setup_inputs(seed: int = 0) -> dict:
    splits = jax.random.split(jax.random.key(seed), 7)
    object_field = centred(splits[0], (2, NROWS, NCOLS), 1.0, 6.0, ((1, 4), (2, 8)), jnp.float32)
    probe = centred(splits[1], (2, PATCH, PATCH), 0.7, 4.0, (), jnp.float32)
    frames = jnp.clip(jnp.exp(math.log(5.0) - 3.218876 * jax.random.uniform(splits[2], (TROWS, TCOLS, TCOLS, SLOT, PATCH, PATCH), jnp.float32) ** shard_levels(splits[2], (TROWS, TCOLS, TCOLS, SLOT, PATCH, PATCH), ((0, 4), (1, 8)), -0.2, 0.2)), 0.2, 5.0)
    positions = set_ends(jax.random.randint(splits[3], (TROWS, TCOLS, TASKS, 2), 0 - PATCH // 2, TILE - PATCH // 2 + 1), jax.random.fold_in(splits[3], 1), 0 - PATCH // 2, (TILE - PATCH // 2 + 1) - 1).astype(jnp.int32)
    helpers_keys = jax.random.split(jax.random.fold_in(splits[4], 1), TROWS * TCOLS * TASKS // TASKS)
    helpers_turns = jax.random.permutation(jax.random.fold_in(splits[4], 3), TROWS * TCOLS * TASKS // TASKS)
    helpers = jax.vmap(lambda own, number: shared_out(jax.random.fold_in(splits[4], 2), own, number, TASKS, TCOLS, 1, SLOT, 2))(helpers_keys, helpers_turns).reshape((TROWS, TCOLS, TASKS, 1))
    task_counts = draw_task_counts(jax.random.fold_in(splits[6], 71), 0)
    return {"object_field": object_field, "probe": probe, "frames": frames, "positions": positions, "helpers": helpers, "task_counts": task_counts}


step_size = 0.1
ridge = 0.5

def dft_tables(length):
    index = jnp.arange(length, dtype=jnp.int32)
    phase = index[:, None] * index[None, :] % length
    angle = 2.0 * jnp.pi / length * phase.astype(jnp.float32)
    factor = length ** (-0.5)
    return (jnp.cos(angle) * factor, -jnp.sin(angle) * factor)

def right_mul(real_in, imag_in, table_re, table_im):
    highest = lax.Precision.HIGHEST
    first = jnp.einsum('bij,jk->bik', real_in, table_re, precision=highest)
    second = jnp.einsum('bij,jk->bik', imag_in, table_im, precision=highest)
    third = jnp.einsum('bij,jk->bik', real_in + imag_in, table_re + table_im, precision=highest)
    return (first - second, third - first - second)

def left_mul(table_re, table_im, real_in, imag_in):
    highest = lax.Precision.HIGHEST
    first = jnp.einsum('ij,bjk->bik', table_re, real_in, precision=highest)
    second = jnp.einsum('ij,bjk->bik', table_im, imag_in, precision=highest)
    third = jnp.einsum('ij,bjk->bik', table_re + table_im, real_in + imag_in, precision=highest)
    return (first - second, third - first - second)

def transform(real_in, imag_in, table_re, table_im):
    mid_re, mid_im = right_mul(real_in, imag_in, table_re, table_im)
    return left_mul(table_re, table_im, mid_re, mid_im)

def task_grad(patches, measured, probe):
    length = patches.shape[-1]
    table_re, table_im = dft_tables(length)
    table_re = table_re.astype(patches.dtype)
    table_im = table_im.astype(patches.dtype)
    probe_re, probe_im = (probe[0], probe[1])
    obj_re, obj_im = (patches[:, 0], patches[:, 1])
    wave_re = probe_re * obj_re - probe_im * obj_im
    wave_im = probe_re * obj_im + probe_im * obj_re
    far_re, far_im = transform(wave_re, wave_im, table_re, table_im)
    weight = far_re * far_re + far_im * far_im - measured
    back_re, back_im = transform(weight * far_re, weight * far_im, table_re, -table_im)
    grad_re = probe_re * back_re + probe_im * back_im
    grad_im = probe_re * back_im - probe_im * back_re
    return jnp.stack([grad_re, grad_im], axis=1)

def reference(object_field, probe, frames, positions, helpers, task_counts):
    half = PATCH // 2
    padded = jnp.pad(object_field, ((0, 0), (half, half), (half, half)))
    task_ids = jnp.arange(TASKS, dtype=jnp.int32)
    helper_cols = helpers[..., 0].astype(jnp.int32)
    same = helper_cols[..., :, None] == helper_cols[..., None, :]
    earlier = task_ids[None, :] < task_ids[:, None]
    ranks = lax.optimization_barrier(jnp.sum(jnp.logical_and(same, earlier), axis=-1)).astype(jnp.int32)
    valid = task_ids < task_counts[..., None]
    row_ids = jnp.broadcast_to(jnp.arange(TROWS, dtype=jnp.int32)[:, None, None], (TROWS, TCOLS, TASKS))
    col_ids = jnp.broadcast_to(jnp.arange(TCOLS, dtype=jnp.int32)[None, :, None], (TROWS, TCOLS, TASKS))
    listing = (row_ids.reshape(-1), col_ids.reshape(-1), positions[..., 0].astype(jnp.int32).reshape(-1), positions[..., 1].astype(jnp.int32).reshape(-1), helper_cols.reshape(-1), ranks.reshape(-1), valid.reshape(-1))
    zero = jnp.int32(0)

    def one_task(grad, item):
        row, col, off_y, off_x, helper, rank, live = item
        start_y = (row * TILE + off_y + half).astype(jnp.int32)
        start_x = (col * TILE + off_x + half).astype(jnp.int32)
        patch = lax.dynamic_slice(padded, (zero, start_y, start_x), (2, PATCH, PATCH))
        patch = patch * live.astype(padded.dtype)
        measured = frames[row, helper, col, rank]
        piece = task_grad(patch[None], measured[None], probe)[0]
        current = lax.dynamic_slice(grad, (zero, start_y, start_x), (2, PATCH, PATCH))
        return (lax.dynamic_update_slice(grad, current + piece, (zero, start_y, start_x)), None)
    grad, unused = lax.scan(one_task, jnp.zeros_like(padded), listing)
    gradient = grad[:, half:half + NROWS, half:half + NCOLS]
    return object_field - step_size * (gradient + ridge * object_field)
```

```python
import functools

import jax
import jax.numpy as jnp
import numpy as np
from jax import lax
from jax.experimental import pallas as pl
from jax.experimental.pallas import tpu as pltpu
from jax.sharding import PartitionSpec as P

step_size = 0.1
ridge = 0.5
f32 = jnp.float32
bf16 = jnp.bfloat16


def split_np(table):
    hi = table.astype(jnp.bfloat16)
    lo = (table - hi.astype(np.float64)).astype(jnp.bfloat16)
    return hi, lo


def dft_tables(length):
    half = length // 2
    n = np.arange(half)[:, None]
    rights, lefts = [], []
    for parity in (0, 1):
        k = 2 * np.arange(half)[None, :] + parity
        angle = -2.0 * np.pi / length * ((n * k) % length)
        re, im = np.cos(angle) * length**-0.5, np.sin(angle) * length**-0.5
        right = np.block([[re, im], [-im, re]])
        hi, lo = split_np(right)
        rights.append(np.concatenate([hi, hi, lo], axis=0))
        hi, lo = split_np(right.T)
        lefts.append(np.concatenate([hi, hi, lo], axis=0))
    right = np.stack(rights)
    right_t = np.stack(lefts)
    left = np.stack([t.T for t in rights])
    left_t = np.stack([t.T for t in lefts])
    perm = np.zeros((length, length))
    order = np.concatenate([np.arange(0, length, 2), np.arange(1, length, 2)])
    perm[order, np.arange(length)] = 1.0
    perm = perm.astype(jnp.bfloat16)
    return right, right_t, left, left_t, np.concatenate([perm, perm], axis=0)


def halves(x):
    hi = x.astype(bf16)
    return hi, (x - hi.astype(f32)).astype(bf16)


def mul_right(x, table):
    hi, lo = halves(x)
    return jnp.dot(jnp.concatenate([hi, lo, hi], axis=1), table, preferred_element_type=f32)


def mul_left(table, x):
    hi, lo = halves(x)
    return jnp.dot(table, jnp.concatenate([hi, lo, hi], axis=0), preferred_element_type=f32)


def masks(a_y, a_x, size):
    rows = lax.broadcasted_iota(jnp.int32, (size, size), 0) >= a_y
    cols = lax.broadcasted_iota(jnp.int32, (size, size), 1) >= a_x
    return rows, cols


def rolled_probe(probe_ref, a_y, a_x):
    return [
        pltpu.roll(pltpu.roll(probe_ref[part], a_x, 1), a_y, 0) for part in range(2)
    ]


def place(info_ref, index, size, blocks):
    start_y, start_x = info_ref[0, index], info_ref[1, index]
    k_y, k_x = start_y // size, start_x // size
    ys = (k_y, jnp.minimum(k_y + 1, blocks - 1))
    xs = (k_x, jnp.minimum(k_x + 1, blocks - 1))
    return ys, xs, start_y - k_y * size, start_x - k_x * size


def window(ref, part, y, x, size):
    return ref.at[
        part, pl.ds(pl.multiple_of(y * size, size), size), pl.ds(pl.multiple_of(x * size, size), size)
    ]


def forward_kernel(blocks, info_ref, field_ref, probe_ref, right_ref, left_ref, far_ref):
    size = probe_ref.shape[1]
    half = size // 2
    index = pl.program_id(0)

    @pl.when(info_ref[2, index] > 0)
    def _():
        ys, xs, a_y, a_x = place(info_ref, index, size, blocks)
        rows, cols = masks(a_y, a_x, size)
        obj = []
        for part in range(2):
            first = jnp.where(cols, window(field_ref, part, ys[0], xs[0], size)[...],
                              window(field_ref, part, ys[0], xs[1], size)[...])
            second = jnp.where(cols, window(field_ref, part, ys[1], xs[0], size)[...],
                               window(field_ref, part, ys[1], xs[1], size)[...])
            obj.append(jnp.where(rows, first, second))
        p_re, p_im = rolled_probe(probe_ref, a_y, a_x)
        re = p_re * obj[0] - p_im * obj[1]
        im = p_re * obj[1] + p_im * obj[0]
        even = mul_right(
            jnp.concatenate([re[:, :half] + re[:, half:], im[:, :half] + im[:, half:]], axis=1), right_ref[0]
        )
        odd = mul_right(
            jnp.concatenate([re[:, :half] - re[:, half:], im[:, :half] - im[:, half:]], axis=1), right_ref[1]
        )
        re = jnp.concatenate([even[:, :half], odd[:, :half]], axis=1)
        im = jnp.concatenate([even[:, half:], odd[:, half:]], axis=1)
        far_ref[0, 0] = mul_left(
            left_ref[0], jnp.concatenate([re[:half] + re[half:], im[:half] + im[half:]], axis=0)
        )
        far_ref[0, 1] = mul_left(
            left_ref[1], jnp.concatenate([re[:half] - re[half:], im[:half] - im[half:]], axis=0)
        )


def backward_kernel(
    blocks, info_ref, far_ref, frame_ref, probe_ref, right_ref, left_ref, perm_ref, grad_ref, sorted_ref
):
    size = probe_ref.shape[1]
    half = size // 2
    index = pl.program_id(0)

    @pl.when(index == 0)
    def _():
        grad_ref[...] = jnp.zeros_like(grad_ref)

    @pl.when(info_ref[2, index] > 0)
    def _():
        ys, xs, a_y, a_x = place(info_ref, index, size, blocks)
        hi, lo = halves(frame_ref[0])
        frame = jnp.dot(jnp.concatenate([hi, lo], axis=1), perm_ref[...], preferred_element_type=f32)
        sorted_ref[0] = frame[:, :half]
        sorted_ref[1] = frame[:, half:]
        back = []
        for parity in range(2):
            frame = jnp.concatenate(
                [sorted_ref[col, pl.ds(parity, half, stride=2), :] for col in range(2)], axis=1
            )
            far = far_ref[0, parity]
            re, im = far[:half], far[half:]
            weight = re * re + im * im - frame
            back.append(mul_left(left_ref[parity], jnp.concatenate([weight * re, weight * im], axis=0)))
        top, bottom = back[0] + back[1], back[0] - back[1]
        re = jnp.concatenate([top[:half], bottom[:half]], axis=0)
        im = jnp.concatenate([top[half:], bottom[half:]], axis=0)
        even = mul_right(jnp.concatenate([re[:, :half], im[:, :half]], axis=1), right_ref[0])
        odd = mul_right(jnp.concatenate([re[:, half:], im[:, half:]], axis=1), right_ref[1])
        low, high = even + odd, even - odd
        re = jnp.concatenate([low[:, :half], high[:, :half]], axis=1)
        im = jnp.concatenate([low[:, half:], high[:, half:]], axis=1)
        p_re, p_im = rolled_probe(probe_ref, a_y, a_x)
        grads = (p_re * re + p_im * im, p_re * im - p_im * re)
        rows, cols = masks(a_y, a_x, size)
        for part in range(2):
            for row in range(2):
                for col in range(2):
                    keep = jnp.logical_and(rows == (row == 0), cols == (col == 0))
                    where = window(grad_ref, part, ys[row], xs[col], size)
                    where[...] += jnp.where(keep, grads[part], 0.0)


def whole(shape):
    return pl.BlockSpec(shape, lambda i, *refs: (0,) * len(shape))


def run_forward(info, field, probe, right, left):
    count, size = info.shape[1], probe.shape[1]
    return pl.pallas_call(
        functools.partial(forward_kernel, field.shape[1] // size),
        out_shape=jax.ShapeDtypeStruct((count, 2, size, size), f32),
        grid_spec=pltpu.PrefetchScalarGridSpec(
            num_scalar_prefetch=1,
            grid=(count,),
            in_specs=[whole(field.shape), whole(probe.shape), whole(right.shape), whole(left.shape)],
            out_specs=pl.BlockSpec((1, 2, size, size), lambda i, *refs: (i, 0, 0, 0)),
        ),
        compiler_params=pltpu.CompilerParams(vmem_limit_bytes=40 << 20),
        cost_estimate=pl.CostEstimate(
            flops=count * 24 * size**3, bytes_accessed=4 * (field.size + count * 2 * size**2), transcendentals=0
        ),
        name="forward",
    )(info, field, probe, right, left)


def run_backward(info, far, frames, probe, right, left, perm, extent):
    count, size = info.shape[1], probe.shape[1]
    return pl.pallas_call(
        functools.partial(backward_kernel, extent // size),
        out_shape=jax.ShapeDtypeStruct((2, extent, extent), f32),
        grid_spec=pltpu.PrefetchScalarGridSpec(
            num_scalar_prefetch=1,
            grid=(count,),
            in_specs=[
                pl.BlockSpec((1, 2, size, size), lambda i, info: (i, 0, 0, 0)),
                pl.BlockSpec((1, size, size), lambda i, info: (info[3, i], 0, 0)),
                whole(probe.shape), whole(right.shape), whole(left.shape), whole(perm.shape),
            ],
            out_specs=whole((2, extent, extent)),
            scratch_shapes=[pltpu.VMEM((2, size, size // 2), f32)],
        ),
        compiler_params=pltpu.CompilerParams(vmem_limit_bytes=40 << 20),
        cost_estimate=pl.CostEstimate(
            flops=count * 24 * size**3, bytes_accessed=4 * count * 3 * size**2, transcendentals=0
        ),
        name="backward",
    )(info, far, frames, probe, right, left, perm)


def from_sides(low_part, high_part, axis):
    count = lax.axis_size(axis)
    forward = [(i, i + 1) for i in range(count - 1)]
    backward = [(target, source) for source, target in forward]
    return lax.ppermute(high_part, axis, forward), lax.ppermute(low_part, axis, backward)


def per_device(object_field, probe, frames, positions, helpers, task_counts):
    tile, size = object_field.shape[1], probe.shape[1]
    half = size // 2
    extent = tile + 2 * half
    kept = frames[0, 0]
    sources, slots = kept.shape[:2]
    fetched = lax.all_to_all(kept, "gx", split_axis=0, concat_axis=0, tiled=True)
    fetched = fetched.reshape(sources * slots, size, size)

    before, after = from_sides(object_field[:, :, :half], object_field[:, :, tile - half :], "gx")
    field = jnp.concatenate([before, object_field, after], axis=2)
    before, after = from_sides(field[:, :half], field[:, tile - half :], "gy")
    field = jnp.concatenate([before, field, after], axis=1)

    offsets = positions[0, 0]
    tasks = offsets.shape[0]
    task_ids = jnp.arange(tasks, dtype=jnp.int32)
    valid = task_ids < task_counts[0, 0]
    helper_cols = helpers[0, 0, :, 0]
    same = helper_cols[:, None] == helper_cols[None, :]
    ranks = jnp.sum(jnp.logical_and(same, task_ids[None, :] < task_ids[:, None]), axis=1)
    info = jnp.stack(
        [offsets[:, 0] + half, offsets[:, 1] + half, valid.astype(jnp.int32), helper_cols * slots + ranks]
    ).astype(jnp.int32)

    right, right_t, left, left_t, perm = (jnp.asarray(t) for t in dft_tables(size))
    far = run_forward(info, field, probe, right, left)
    summed = run_backward(info, far, fetched, probe, right_t, left_t, perm, extent)

    before, after = from_sides(summed[:, :, :half], summed[:, :, tile + half :], "gx")
    middle = summed[:, :, half : half + tile]
    middle = middle.at[:, :, :half].add(before)
    middle = middle.at[:, :, tile - half :].add(after)
    before, after = from_sides(middle[:, :half], middle[:, tile + half :], "gy")
    gradient = middle[:, half : half + tile]
    gradient = gradient.at[:, :half].add(before)
    gradient = gradient.at[:, tile - half :].add(after)
    return object_field - step_size * (gradient + ridge * object_field)


def solution(mesh):
    in_specs = (
        P(None, "gy", "gx"),
        P(),
        P("gy", "gx", None, None, None, None),
        P("gy", "gx", None, None),
        P("gy", "gx", None, None),
        P("gy", "gx"),
    )
    out_specs = P(None, "gy", "gx")
    return jax.shard_map(
        per_device, mesh=mesh, in_specs=in_specs, out_specs=out_specs, check_vma=False
    )
```

```python
import functools

import jax
import jax.numpy as jnp
import numpy as np
from jax import lax
from jax.experimental import pallas as pl
from jax.experimental.pallas import tpu as pltpu
from jax.sharding import PartitionSpec as P

step_size = 0.1
ridge = 0.5
f32 = jnp.float32
bf16 = jnp.bfloat16


def split_np(table):
    hi = table.astype(jnp.bfloat16)
    lo = (table - hi.astype(np.float64)).astype(jnp.bfloat16)
    return hi, lo


def dft_tables(length):
    half = length // 2
    n = np.arange(half)[:, None]
    rights, lefts = [], []
    for parity in (0, 1):
        k = 2 * np.arange(half)[None, :] + parity
        angle = -2.0 * np.pi / length * ((n * k) % length)
        re, im = np.cos(angle) * length**-0.5, np.sin(angle) * length**-0.5
        right = np.block([[re, im], [-im, re]])
        hi, lo = split_np(right)
        rights.append(np.concatenate([hi, hi, lo], axis=0))
        hi, lo = split_np(right.T)
        lefts.append(np.concatenate([hi, hi, lo], axis=0))
    right = np.stack(rights)
    right_t = np.stack(lefts)
    left = np.stack([t.T for t in rights])
    left_t = np.stack([t.T for t in lefts])
    perm = np.zeros((length, length))
    order = np.concatenate([np.arange(0, length, 2), np.arange(1, length, 2)])
    perm[order, np.arange(length)] = 1.0
    perm = perm.astype(jnp.bfloat16)
    return right, right_t, left, left_t, np.concatenate([perm, perm], axis=0)


def halves(x):
    hi = x.astype(bf16)
    return hi, (x - hi.astype(f32)).astype(bf16)


def mul_right(x, table):
    hi, lo = halves(x)
    return jnp.dot(jnp.concatenate([hi, lo, hi], axis=1), table, preferred_element_type=f32)


def mul_left(table, x):
    hi, lo = halves(x)
    return jnp.dot(table, jnp.concatenate([hi, lo, hi], axis=0), preferred_element_type=f32)


def masks(a_y, a_x, size):
    rows = lax.broadcasted_iota(jnp.int32, (size, size), 0) >= a_y
    cols = lax.broadcasted_iota(jnp.int32, (size, size), 1) >= a_x
    return rows, cols


def rolled_probe(probe_ref, a_y, a_x):
    return [
        pltpu.roll(pltpu.roll(probe_ref[part], a_x, 1), a_y, 0) for part in range(2)
    ]


def place(info_ref, index, size, blocks):
    start_y, start_x = info_ref[0, index], info_ref[1, index]
    k_y, k_x = start_y // size, start_x // size
    ys = (k_y, jnp.minimum(k_y + 1, blocks - 1))
    xs = (k_x, jnp.minimum(k_x + 1, blocks - 1))
    return ys, xs, start_y - k_y * size, start_x - k_x * size


def window(ref, part, y, x, size):
    return ref.at[
        part, pl.ds(pl.multiple_of(y * size, size), size), pl.ds(pl.multiple_of(x * size, size), size)
    ]


def forward_kernel(blocks, info_ref, field_ref, probe_ref, right_ref, left_ref, far_ref):
    size = probe_ref.shape[1]
    half = size // 2
    index = pl.program_id(0)

    @pl.when(info_ref[2, index] > 0)
    def _():
        ys, xs, a_y, a_x = place(info_ref, index, size, blocks)
        rows, cols = masks(a_y, a_x, size)
        obj = []
        for part in range(2):
            first = jnp.where(cols, window(field_ref, part, ys[0], xs[0], size)[...],
                              window(field_ref, part, ys[0], xs[1], size)[...])
            second = jnp.where(cols, window(field_ref, part, ys[1], xs[0], size)[...],
                               window(field_ref, part, ys[1], xs[1], size)[...])
            obj.append(jnp.where(rows, first, second))
        p_re, p_im = rolled_probe(probe_ref, a_y, a_x)
        re = p_re * obj[0] - p_im * obj[1]
        im = p_re * obj[1] + p_im * obj[0]
        even = mul_right(
            jnp.concatenate([re[:, :half] + re[:, half:], im[:, :half] + im[:, half:]], axis=1), right_ref[0]
        )
        odd = mul_right(
            jnp.concatenate([re[:, :half] - re[:, half:], im[:, :half] - im[:, half:]], axis=1), right_ref[1]
        )
        re = jnp.concatenate([even[:, :half], odd[:, :half]], axis=1)
        im = jnp.concatenate([even[:, half:], odd[:, half:]], axis=1)
        far_ref[0, 0] = mul_left(
            left_ref[0], jnp.concatenate([re[:half] + re[half:], im[:half] + im[half:]], axis=0)
        )
        far_ref[0, 1] = mul_left(
            left_ref[1], jnp.concatenate([re[:half] - re[half:], im[:half] - im[half:]], axis=0)
        )


def backward_kernel(blocks, chunks, begun, info_ref, far_ref, *refs):
    frame_refs, refs = refs[:chunks], refs[chunks:]
    probe_ref, right_ref, left_ref, perm_ref = refs[:4]
    grad_ref, sorted_ref, frame_ref = refs[-3:]
    slots = pl.num_programs(0) // chunks
    size = probe_ref.shape[1]
    half = size // 2
    index = pl.program_id(0)

    @pl.when(index == 0)
    def _():
        grad_ref[...] = refs[4][...] if begun else jnp.zeros_like(grad_ref)

    for chunk in range(chunks):

        @pl.when(index // slots == chunk)
        def _():
            frame_ref[...] = frame_refs[chunk][0]

    @pl.when(info_ref[2, index] > 0)
    def _():
        ys, xs, a_y, a_x = place(info_ref, index, size, blocks)
        hi, lo = halves(frame_ref[...])
        frame = jnp.dot(jnp.concatenate([hi, lo], axis=1), perm_ref[...], preferred_element_type=f32)
        sorted_ref[0] = frame[:, :half]
        sorted_ref[1] = frame[:, half:]
        back = []
        for parity in range(2):
            frame = jnp.concatenate(
                [sorted_ref[col, pl.ds(parity, half, stride=2), :] for col in range(2)], axis=1
            )
            far = far_ref[0, parity]
            re, im = far[:half], far[half:]
            weight = re * re + im * im - frame
            back.append(mul_left(left_ref[parity], jnp.concatenate([weight * re, weight * im], axis=0)))
        top, bottom = back[0] + back[1], back[0] - back[1]
        re = jnp.concatenate([top[:half], bottom[:half]], axis=0)
        im = jnp.concatenate([top[half:], bottom[half:]], axis=0)
        even = mul_right(jnp.concatenate([re[:, :half], im[:, :half]], axis=1), right_ref[0])
        odd = mul_right(jnp.concatenate([re[:, half:], im[:, half:]], axis=1), right_ref[1])
        low, high = even + odd, even - odd
        re = jnp.concatenate([low[:, :half], high[:, :half]], axis=1)
        im = jnp.concatenate([low[:, half:], high[:, half:]], axis=1)
        p_re, p_im = rolled_probe(probe_ref, a_y, a_x)
        grads = (p_re * re + p_im * im, p_re * im - p_im * re)
        rows, cols = masks(a_y, a_x, size)
        for part in range(2):
            for row in range(2):
                for col in range(2):
                    keep = jnp.logical_and(rows == (row == 0), cols == (col == 0))
                    where = window(grad_ref, part, ys[row], xs[col], size)
                    where[...] += jnp.where(keep, grads[part], 0.0)


def whole(shape):
    return pl.BlockSpec(shape, lambda i, *refs: (0,) * len(shape))


def run_forward(info, field, probe, right, left):
    count, size = info.shape[1], probe.shape[1]
    return pl.pallas_call(
        functools.partial(forward_kernel, field.shape[1] // size),
        out_shape=jax.ShapeDtypeStruct((count, 2, size, size), f32),
        grid_spec=pltpu.PrefetchScalarGridSpec(
            num_scalar_prefetch=1,
            grid=(count,),
            in_specs=[whole(field.shape), whole(probe.shape), whole(right.shape), whole(left.shape)],
            out_specs=pl.BlockSpec((1, 2, size, size), lambda i, *refs: (i, 0, 0, 0)),
        ),
        compiler_params=pltpu.CompilerParams(vmem_limit_bytes=40 << 20),
        cost_estimate=pl.CostEstimate(
            flops=count * 24 * size**3, bytes_accessed=4 * (field.size + count * 2 * size**2), transcendentals=0
        ),
        name="forward",
    )(info, field, probe, right, left)


def run_backward(info, first, far, frames, probe, right, left, perm, extent, grad):
    slots, size = frames[0].shape[:2]
    count = slots * len(frames)
    tables = [probe, right, left, perm] + ([] if grad is None else [grad])

    def frame_spec(chunk):
        return pl.BlockSpec(
            (1, size, size), lambda i, info: (jnp.clip(i - chunk * slots, 0, slots - 1), 0, 0)
        )

    return pl.pallas_call(
        functools.partial(backward_kernel, extent // size, len(frames), grad is not None),
        out_shape=jax.ShapeDtypeStruct((2, extent, extent), f32),
        grid_spec=pltpu.PrefetchScalarGridSpec(
            num_scalar_prefetch=1,
            grid=(count,),
            in_specs=[pl.BlockSpec((1, 2, size, size), lambda i, info: (first + i, 0, 0, 0))]
            + [frame_spec(chunk) for chunk in range(len(frames))]
            + [whole(table.shape) for table in tables],
            out_specs=whole((2, extent, extent)),
            scratch_shapes=[pltpu.VMEM((2, size, size // 2), f32), pltpu.VMEM((size, size), f32)],
        ),
        compiler_params=pltpu.CompilerParams(vmem_limit_bytes=40 << 20),
        cost_estimate=pl.CostEstimate(
            flops=count * 24 * size**3, bytes_accessed=4 * count * 3 * size**2, transcendentals=0
        ),
        name="backward",
    )(info[:, first : first + count], far, *frames, *tables)


def from_sides(low_part, high_part, axis):
    count = lax.axis_size(axis)
    forward = [(i, i + 1) for i in range(count - 1)]
    backward = [(target, source) for source, target in forward]
    return lax.ppermute(high_part, axis, forward), lax.ppermute(low_part, axis, backward)


def per_device(object_field, probe, frames, positions, helpers, task_counts):
    tile, size = object_field.shape[1], probe.shape[1]
    half = size // 2
    extent = tile + 2 * half
    kept = frames[0, 0]
    sources, slots = kept.shape[:2]
    me = lax.axis_index("gx")
    paired = sources & (sources - 1) == 0
    ids = list(range(sources))

    def target_of(d, i):
        return i ^ d if paired else (i + d) % sources

    def source_of(d, i):
        return i ^ d if paired else (i - d + sources) % sources

    far_steps, near_steps = ids[sources // 2 :], ids[1 : sources // 2]
    order = []
    for number, d in enumerate(far_steps):
        order += [d] + near_steps[number : number + 1]
    groups = [[0] + order[:2]] + [order[i : i + 2] for i in range(2, len(order), 2)]
    groups = [group for group in groups if group]
    order = [d for group in groups for d in group]

    before, after = from_sides(object_field[:, :, :half], object_field[:, :, tile - half :], "gx")
    early = me
    late, before, after = lax.optimization_barrier((me, before, after))
    field = jnp.concatenate([before, object_field, after], axis=2)
    before, after = from_sides(field[:, :half], field[:, tile - half :], "gy")
    field = jnp.concatenate([before, field, after], axis=1)

    offsets = positions[0, 0]
    tasks = offsets.shape[0]
    task_ids = jnp.arange(tasks, dtype=jnp.int32)
    valid = task_ids < task_counts[0, 0]
    helper_cols = helpers[0, 0, :, 0]
    same = helper_cols[:, None] == helper_cols[None, :]
    ranks = jnp.sum(jnp.logical_and(same, task_ids[None, :] < task_ids[:, None]), axis=1)
    slot_of = helper_cols * slots + ranks
    kinds = jnp.concatenate(
        [source_of(d, me) * slots + jnp.arange(slots, dtype=jnp.int32) for d in order]
    )
    hit = jnp.logical_and(slot_of[None, :] == kinds[:, None], valid[None, :]).astype(jnp.int32)
    info = jnp.stack(
        [
            jnp.sum(hit * (offsets[None, :, 0] + half), axis=1),
            jnp.sum(hit * (offsets[None, :, 1] + half), axis=1),
            jnp.sum(hit, axis=1),
        ]
    ).astype(jnp.int32)

    right, right_t, left, left_t, perm = (jnp.asarray(t) for t in dft_tables(size))
    far = run_forward(info, field, probe, right, left)
    arrived = {}
    for number, d in enumerate(order):
        at = early if number < 3 else late
        if number >= 5:
            past = order[number - 4]
            at, arrived[past] = lax.optimization_barrier((at, arrived[past]))
        chunk = lax.dynamic_index_in_dim(kept, target_of(d, at), axis=0, keepdims=False)
        arrived[d] = chunk if d == 0 else lax.ppermute(chunk, "gx", [(i, target_of(d, i)) for i in ids])

    summed, first = None, 0
    for group in groups:
        summed = run_backward(
            info, first, far, [arrived[d] for d in group], probe, right_t, left_t, perm, extent, summed
        )
        first += len(group) * slots

    west, east = from_sides(summed[:, :, :half], summed[:, :, tile + half :], "gx")
    inner = summed[:, :, half : half + tile]
    north, south = from_sides(inner[:, :half], inner[:, tile + half :], "gy")
    corners = jnp.concatenate([west, east], axis=2)
    corner_north, corner_south = from_sides(corners[:, :half], corners[:, tile + half :], "gy")
    gradient = inner[:, half : half + tile]
    gradient = gradient.at[:, :half].add(north)
    gradient = gradient.at[:, tile - half :].add(south)
    side = corners[:, half : half + tile]
    side = side.at[:, :half].add(corner_north)
    side = side.at[:, tile - half :].add(corner_south)
    gradient = gradient.at[:, :, :half].add(side[:, :, :half])
    gradient = gradient.at[:, :, tile - half :].add(side[:, :, half:])
    return object_field - step_size * (gradient + ridge * object_field)


def solution(mesh):
    in_specs = (
        P(None, "gy", "gx"),
        P(),
        P("gy", "gx", None, None, None, None),
        P("gy", "gx", None, None),
        P("gy", "gx", None, None),
        P("gy", "gx"),
    )
    out_specs = P(None, "gy", "gx")
    return jax.shard_map(
        per_device, mesh=mesh, in_specs=in_specs, out_specs=out_specs, check_vma=False
    )
```

```python
import functools

import jax
import jax.numpy as jnp
import numpy as np
from jax import lax
from jax.experimental import pallas as pl
from jax.experimental.pallas import tpu as pltpu
from jax.sharding import PartitionSpec as P

step_size = 0.1
ridge = 0.5
f32 = jnp.float32
bf16 = jnp.bfloat16


def split_np(table):
    hi = table.astype(jnp.bfloat16)
    lo = (table - hi.astype(np.float64)).astype(jnp.bfloat16)
    return hi, lo


def dft_tables(length):
    half = length // 2
    n = np.arange(half)[:, None]
    rights, lefts = [], []
    for parity in (0, 1):
        k = 2 * np.arange(half)[None, :] + parity
        angle = -2.0 * np.pi / length * ((n * k) % length)
        re, im = np.cos(angle) * length**-0.5, np.sin(angle) * length**-0.5
        right = np.block([[re, im], [-im, re]])
        hi, lo = split_np(right)
        rights.append(np.concatenate([hi, hi, lo], axis=0))
        hi, lo = split_np(right.T)
        lefts.append(np.concatenate([hi, hi, lo], axis=0))
    right = np.stack(rights)
    right_t = np.stack(lefts)
    left = np.stack([t.T for t in rights])
    left_t = np.stack([t.T for t in lefts])
    perm = np.zeros((length, length))
    order = np.concatenate([np.arange(0, length, 2), np.arange(1, length, 2)])
    perm[order, np.arange(length)] = 1.0
    perm = perm.astype(jnp.bfloat16)
    return right, right_t, left, left_t, np.concatenate([perm, perm], axis=0)


def halves(x):
    hi = x.astype(bf16)
    return hi, (x - hi.astype(f32)).astype(bf16)


def mul_right(x, table):
    hi, lo = halves(x)
    return jnp.dot(jnp.concatenate([hi, lo, hi], axis=1), table, preferred_element_type=f32)


def mul_left(table, x):
    hi, lo = halves(x)
    return jnp.dot(table, jnp.concatenate([hi, lo, hi], axis=0), preferred_element_type=f32)


def masks(a_y, a_x, size):
    rows = lax.broadcasted_iota(jnp.int32, (size, size), 0) >= a_y
    cols = lax.broadcasted_iota(jnp.int32, (size, size), 1) >= a_x
    return rows, cols


def rolled_probe(probe_ref, a_y, a_x):
    return [
        pltpu.roll(pltpu.roll(probe_ref[part], a_x, 1), a_y, 0) for part in range(2)
    ]


def place(info_ref, index, size, blocks):
    start_y, start_x = info_ref[0, index], info_ref[1, index]
    k_y, k_x = start_y // size, start_x // size
    ys = (k_y, jnp.minimum(k_y + 1, blocks - 1))
    xs = (k_x, jnp.minimum(k_x + 1, blocks - 1))
    return ys, xs, start_y - k_y * size, start_x - k_x * size


def window(ref, part, y, x, size):
    return ref.at[
        part, pl.ds(pl.multiple_of(y * size, size), size), pl.ds(pl.multiple_of(x * size, size), size)
    ]


def forward_kernel(blocks, info_ref, field_ref, probe_ref, right_ref, left_ref, far_ref):
    size = probe_ref.shape[1]
    half = size // 2
    index = pl.program_id(0)

    @pl.when(info_ref[2, index] > 0)
    def _():
        ys, xs, a_y, a_x = place(info_ref, index, size, blocks)
        rows, cols = masks(a_y, a_x, size)
        obj = []
        for part in range(2):
            first = jnp.where(cols, window(field_ref, part, ys[0], xs[0], size)[...],
                              window(field_ref, part, ys[0], xs[1], size)[...])
            second = jnp.where(cols, window(field_ref, part, ys[1], xs[0], size)[...],
                               window(field_ref, part, ys[1], xs[1], size)[...])
            obj.append(jnp.where(rows, first, second))
        p_re, p_im = rolled_probe(probe_ref, a_y, a_x)
        re = p_re * obj[0] - p_im * obj[1]
        im = p_re * obj[1] + p_im * obj[0]
        even = mul_right(
            jnp.concatenate([re[:, :half] + re[:, half:], im[:, :half] + im[:, half:]], axis=1), right_ref[0]
        )
        odd = mul_right(
            jnp.concatenate([re[:, :half] - re[:, half:], im[:, :half] - im[:, half:]], axis=1), right_ref[1]
        )
        re = jnp.concatenate([even[:, :half], odd[:, :half]], axis=1)
        im = jnp.concatenate([even[:, half:], odd[:, half:]], axis=1)
        far_ref[0, 0] = mul_left(
            left_ref[0], jnp.concatenate([re[:half] + re[half:], im[:half] + im[half:]], axis=0)
        )
        far_ref[0, 1] = mul_left(
            left_ref[1], jnp.concatenate([re[:half] - re[half:], im[:half] - im[half:]], axis=0)
        )


def backward_kernel(blocks, chunks, begun, info_ref, far_ref, *refs):
    frame_refs, refs = refs[:chunks], refs[chunks:]
    probe_ref, right_ref, left_ref, perm_ref = refs[:4]
    grad_ref, sorted_ref, frame_ref = refs[-3:]
    slots = pl.num_programs(0) // chunks
    size = probe_ref.shape[1]
    half = size // 2
    index = pl.program_id(0)

    @pl.when(index == 0)
    def _():
        grad_ref[...] = refs[4][...] if begun else jnp.zeros_like(grad_ref)

    for chunk in range(chunks):

        @pl.when(index // slots == chunk)
        def _():
            frame_ref[...] = frame_refs[chunk][0]

    @pl.when(info_ref[2, index] > 0)
    def _():
        ys, xs, a_y, a_x = place(info_ref, index, size, blocks)
        hi, lo = halves(frame_ref[...])
        frame = jnp.dot(jnp.concatenate([hi, lo], axis=1), perm_ref[...], preferred_element_type=f32)
        sorted_ref[0] = frame[:, :half]
        sorted_ref[1] = frame[:, half:]
        back = []
        for parity in range(2):
            frame = jnp.concatenate(
                [sorted_ref[col, pl.ds(parity, half, stride=2), :] for col in range(2)], axis=1
            )
            far = far_ref[0, parity]
            re, im = far[:half], far[half:]
            weight = re * re + im * im - frame
            back.append(mul_left(left_ref[parity], jnp.concatenate([weight * re, weight * im], axis=0)))
        top, bottom = back[0] + back[1], back[0] - back[1]
        re = jnp.concatenate([top[:half], bottom[:half]], axis=0)
        im = jnp.concatenate([top[half:], bottom[half:]], axis=0)
        even = mul_right(jnp.concatenate([re[:, :half], im[:, :half]], axis=1), right_ref[0])
        odd = mul_right(jnp.concatenate([re[:, half:], im[:, half:]], axis=1), right_ref[1])
        low, high = even + odd, even - odd
        re = jnp.concatenate([low[:, :half], high[:, :half]], axis=1)
        im = jnp.concatenate([low[:, half:], high[:, half:]], axis=1)
        p_re, p_im = rolled_probe(probe_ref, a_y, a_x)
        grads = (p_re * re + p_im * im, p_re * im - p_im * re)
        rows, cols = masks(a_y, a_x, size)
        for part in range(2):
            for row in range(2):
                for col in range(2):
                    keep = jnp.logical_and(rows == (row == 0), cols == (col == 0))
                    where = window(grad_ref, part, ys[row], xs[col], size)
                    where[...] += jnp.where(keep, grads[part], 0.0)


def whole(shape):
    return pl.BlockSpec(shape, lambda i, *refs: (0,) * len(shape))


def run_forward(info, field, probe, right, left):
    count, size = info.shape[1], probe.shape[1]
    return pl.pallas_call(
        functools.partial(forward_kernel, field.shape[1] // size),
        out_shape=jax.ShapeDtypeStruct((count, 2, size, size), f32),
        grid_spec=pltpu.PrefetchScalarGridSpec(
            num_scalar_prefetch=1,
            grid=(count,),
            in_specs=[whole(field.shape), whole(probe.shape), whole(right.shape), whole(left.shape)],
            out_specs=pl.BlockSpec((1, 2, size, size), lambda i, *refs: (i, 0, 0, 0)),
        ),
        compiler_params=pltpu.CompilerParams(vmem_limit_bytes=40 << 20),
        cost_estimate=pl.CostEstimate(
            flops=count * 24 * size**3, bytes_accessed=4 * (field.size + count * 2 * size**2), transcendentals=0
        ),
        name="forward",
    )(info, field, probe, right, left)


def run_backward(info, first, far, frames, probe, right, left, perm, extent, grad):
    slots, size = frames[0].shape[:2]
    count = slots * len(frames)
    tables = [probe, right, left, perm] + ([] if grad is None else [grad])

    def frame_spec(chunk):
        return pl.BlockSpec(
            (1, size, size), lambda i, info: (jnp.clip(i - chunk * slots, 0, slots - 1), 0, 0)
        )

    return pl.pallas_call(
        functools.partial(backward_kernel, extent // size, len(frames), grad is not None),
        out_shape=jax.ShapeDtypeStruct((2, extent, extent), f32),
        grid_spec=pltpu.PrefetchScalarGridSpec(
            num_scalar_prefetch=1,
            grid=(count,),
            in_specs=[pl.BlockSpec((1, 2, size, size), lambda i, info: (first + i, 0, 0, 0))]
            + [frame_spec(chunk) for chunk in range(len(frames))]
            + [whole(table.shape) for table in tables],
            out_specs=whole((2, extent, extent)),
            scratch_shapes=[pltpu.VMEM((2, size, size // 2), f32), pltpu.VMEM((size, size), f32)],
        ),
        compiler_params=pltpu.CompilerParams(vmem_limit_bytes=40 << 20),
        cost_estimate=pl.CostEstimate(
            flops=count * 24 * size**3, bytes_accessed=4 * count * 3 * size**2, transcendentals=0
        ),
        name="backward",
    )(info[:, first : first + count], far, *frames, *tables)


def from_sides(low_part, high_part, axis):
    count = lax.axis_size(axis)
    forward = [(i, i + 1) for i in range(count - 1)]
    backward = [(target, source) for source, target in forward]
    return lax.ppermute(high_part, axis, forward), lax.ppermute(low_part, axis, backward)


def per_device(object_field, probe, frames, positions, helpers, task_counts):
    tile, size = object_field.shape[1], probe.shape[1]
    half = size // 2
    extent = tile + 2 * half
    kept = frames[0, 0]
    sources, slots = kept.shape[:2]
    me = lax.axis_index("gx")
    paired = sources & (sources - 1) == 0
    ids = list(range(sources))

    def target_of(d, i):
        return i ^ d if paired else (i + d) % sources

    def source_of(d, i):
        return i ^ d if paired else (i - d + sources) % sources

    far_steps, near_steps = ids[sources // 2 :], ids[1 : sources // 2]
    order = []
    for number, d in enumerate(far_steps):
        order += [d] + near_steps[number : number + 1]
    groups = [[0] + order[:2]] + [order[i : i + 2] for i in range(2, len(order), 2)]
    groups = [group for group in groups if group]
    order = [d for group in groups for d in group]

    def chunk_of(d, at):
        return lax.dynamic_index_in_dim(kept, target_of(d, at), axis=0, keepdims=False)

    leading, sided = lax.optimization_barrier((chunk_of(order[1], me), object_field))
    before, after = from_sides(sided[:, :, :half], sided[:, :, tile - half :], "gx")
    late, before, after = lax.optimization_barrier((me, before, after))
    field = jnp.concatenate([before, object_field, after], axis=2)
    before, after = from_sides(field[:, :half], field[:, tile - half :], "gy")
    field = jnp.concatenate([before, field, after], axis=1)

    offsets = positions[0, 0]
    tasks = offsets.shape[0]
    task_ids = jnp.arange(tasks, dtype=jnp.int32)
    valid = task_ids < task_counts[0, 0]
    helper_cols = helpers[0, 0, :, 0]
    same = helper_cols[:, None] == helper_cols[None, :]
    ranks = jnp.sum(jnp.logical_and(same, task_ids[None, :] < task_ids[:, None]), axis=1)
    slot_of = helper_cols * slots + ranks
    kinds = jnp.concatenate(
        [source_of(d, me) * slots + jnp.arange(slots, dtype=jnp.int32) for d in order]
    )
    hit = jnp.logical_and(slot_of[None, :] == kinds[:, None], valid[None, :]).astype(jnp.int32)
    info = jnp.stack(
        [
            jnp.sum(hit * (offsets[None, :, 0] + half), axis=1),
            jnp.sum(hit * (offsets[None, :, 1] + half), axis=1),
            jnp.sum(hit, axis=1),
        ]
    ).astype(jnp.int32)

    right, right_t, left, left_t, perm = (jnp.asarray(t) for t in dft_tables(size))
    far = run_forward(info, field, probe, right, left)
    arrived = {}
    for number, d in enumerate(order):
        at = me if d == 0 else late
        if number >= 5:
            past = order[number - 4]
            at, arrived[past] = lax.optimization_barrier((at, arrived[past]))
        chunk = leading if number == 1 else chunk_of(d, at)
        arrived[d] = chunk if d == 0 else lax.ppermute(chunk, "gx", [(i, target_of(d, i)) for i in ids])

    summed, first = None, 0
    for group in groups:
        summed = run_backward(
            info, first, far, [arrived[d] for d in group], probe, right_t, left_t, perm, extent, summed
        )
        first += len(group) * slots

    top, middle, bottom = slice(0, half), slice(half, tile - half), slice(tile - half, tile)
    inner = summed[:, half : half + tile]
    sent = (
        summed[:, :half], summed[:, tile + half :], inner[:, middle, :half], inner[:, middle, tile + half :]
    )
    sent = lax.optimization_barrier(sent)
    north, south = from_sides(sent[0], sent[1], "gy")
    west_mid, east_mid = from_sides(sent[2], sent[3], "gx")
    north, south, west_mid, east_mid = lax.optimization_barrier((north, south, west_mid, east_mid))
    upper, lower = inner[:, top] + north, inner[:, bottom] + south
    ends = jnp.concatenate([upper, lower], axis=1)
    west_ends, east_ends = from_sides(ends[:, :, :half], ends[:, :, tile + half :], "gx")
    west = jnp.concatenate([west_ends[:, :half], west_mid, west_ends[:, half:]], axis=1)
    east = jnp.concatenate([east_ends[:, :half], east_mid, east_ends[:, half:]], axis=1)
    own = slice(half, half + tile)
    gradient = jnp.concatenate([upper[:, :, own], inner[:, middle, own], lower[:, :, own]], axis=1)
    gradient = gradient.at[:, :, :half].add(west)
    gradient = gradient.at[:, :, tile - half :].add(east)
    return object_field - step_size * (gradient + ridge * object_field)


def solution(mesh):
    in_specs = (
        P(None, "gy", "gx"),
        P(),
        P("gy", "gx", None, None, None, None),
        P("gy", "gx", None, None),
        P("gy", "gx", None, None),
        P("gy", "gx"),
    )
    out_specs = P(None, "gy", "gx")
    return jax.shard_map(
        per_device, mesh=mesh, in_specs=in_specs, out_specs=out_specs, check_vma=False
    )
```

```python
import functools

import jax
import jax.numpy as jnp
import numpy as np
from jax import lax
from jax.experimental import pallas as pl
from jax.experimental.pallas import tpu as pltpu
from jax.sharding import PartitionSpec as P

step_size = 0.1
ridge = 0.5
f32 = jnp.float32
bf16 = jnp.bfloat16


def split_np(table):
    hi = table.astype(jnp.bfloat16)
    lo = (table - hi.astype(np.float64)).astype(jnp.bfloat16)
    return hi, lo


def dft_tables(length):
    half = length // 2
    n = np.arange(half)[:, None]
    rights, lefts = [], []
    for parity in (0, 1):
        k = 2 * np.arange(half)[None, :] + parity
        angle = -2.0 * np.pi / length * ((n * k) % length)
        re, im = np.cos(angle) * length**-0.5, np.sin(angle) * length**-0.5
        right = np.block([[re, im], [-im, re]])
        hi, lo = split_np(right)
        rights.append(np.concatenate([hi, hi, lo], axis=0))
        hi, lo = split_np(right.T)
        lefts.append(np.concatenate([hi, hi, lo], axis=0))
    right = np.stack(rights)
    right_t = np.stack(lefts)
    left = np.stack([t.T for t in rights])
    left_t = np.stack([t.T for t in lefts])
    perm = np.zeros((length, length))
    order = np.concatenate([np.arange(0, length, 2), np.arange(1, length, 2)])
    perm[order, np.arange(length)] = 1.0
    perm = perm.astype(jnp.bfloat16)
    return right, right_t, left, left_t, np.concatenate([perm, perm], axis=0)


def halves(x):
    hi = x.astype(bf16)
    return hi, (x - hi.astype(f32)).astype(bf16)


def mul_right(x, table):
    hi, lo = halves(x)
    return jnp.dot(jnp.concatenate([hi, lo, hi], axis=1), table, preferred_element_type=f32)


def mul_left(table, x):
    hi, lo = halves(x)
    return jnp.dot(table, jnp.concatenate([hi, lo, hi], axis=0), preferred_element_type=f32)


def masks(a_y, a_x, size):
    rows = lax.broadcasted_iota(jnp.int32, (size, size), 0) >= a_y
    cols = lax.broadcasted_iota(jnp.int32, (size, size), 1) >= a_x
    return rows, cols


def rolled_probe(probe_ref, a_y, a_x):
    return [
        pltpu.roll(pltpu.roll(probe_ref[part], a_x, 1), a_y, 0) for part in range(2)
    ]


def place(info_ref, index, size, blocks):
    start_y, start_x = info_ref[0, index], info_ref[1, index]
    k_y, k_x = start_y // size, start_x // size
    ys = (k_y, jnp.minimum(k_y + 1, blocks - 1))
    xs = (k_x, jnp.minimum(k_x + 1, blocks - 1))
    return ys, xs, start_y - k_y * size, start_x - k_x * size


def window(ref, part, y, x, size):
    return ref.at[
        part, pl.ds(pl.multiple_of(y * size, size), size), pl.ds(pl.multiple_of(x * size, size), size)
    ]


def forward_kernel(blocks, info_ref, field_ref, probe_ref, right_ref, left_ref, far_ref):
    size = probe_ref.shape[1]
    half = size // 2
    index = pl.program_id(0)

    @pl.when(info_ref[2, index] > 0)
    def _():
        ys, xs, a_y, a_x = place(info_ref, index, size, blocks)
        rows, cols = masks(a_y, a_x, size)
        obj = []
        for part in range(2):
            first = jnp.where(cols, window(field_ref, part, ys[0], xs[0], size)[...],
                              window(field_ref, part, ys[0], xs[1], size)[...])
            second = jnp.where(cols, window(field_ref, part, ys[1], xs[0], size)[...],
                               window(field_ref, part, ys[1], xs[1], size)[...])
            obj.append(jnp.where(rows, first, second))
        p_re, p_im = rolled_probe(probe_ref, a_y, a_x)
        re = p_re * obj[0] - p_im * obj[1]
        im = p_re * obj[1] + p_im * obj[0]
        even = mul_right(
            jnp.concatenate([re[:, :half] + re[:, half:], im[:, :half] + im[:, half:]], axis=1), right_ref[0]
        )
        odd = mul_right(
            jnp.concatenate([re[:, :half] - re[:, half:], im[:, :half] - im[:, half:]], axis=1), right_ref[1]
        )
        re = jnp.concatenate([even[:, :half], odd[:, :half]], axis=1)
        im = jnp.concatenate([even[:, half:], odd[:, half:]], axis=1)
        far_ref[0, 0] = mul_left(
            left_ref[0], jnp.concatenate([re[:half] + re[half:], im[:half] + im[half:]], axis=0)
        )
        far_ref[0, 1] = mul_left(
            left_ref[1], jnp.concatenate([re[:half] - re[half:], im[:half] - im[half:]], axis=0)
        )


def backward_kernel(blocks, chunks, begun, info_ref, far_ref, *refs):
    frame_refs, refs = refs[:chunks], refs[chunks:]
    probe_ref, right_ref, left_ref, perm_ref = refs[:4]
    grad_ref, sorted_ref, frame_ref = refs[-3:]
    slots = pl.num_programs(0) // chunks
    size = probe_ref.shape[1]
    half = size // 2
    index = pl.program_id(0)

    @pl.when(index == 0)
    def _():
        grad_ref[...] = refs[4][...] if begun else jnp.zeros_like(grad_ref)

    for chunk in range(chunks):

        @pl.when(index // slots == chunk)
        def _():
            frame_ref[...] = frame_refs[chunk][0]

    @pl.when(info_ref[2, index] > 0)
    def _():
        ys, xs, a_y, a_x = place(info_ref, index, size, blocks)
        hi, lo = halves(frame_ref[...])
        frame = jnp.dot(jnp.concatenate([hi, lo], axis=1), perm_ref[...], preferred_element_type=f32)
        sorted_ref[0] = frame[:, :half]
        sorted_ref[1] = frame[:, half:]
        back = []
        for parity in range(2):
            frame = jnp.concatenate(
                [sorted_ref[col, pl.ds(parity, half, stride=2), :] for col in range(2)], axis=1
            )
            far = far_ref[0, parity]
            re, im = far[:half], far[half:]
            weight = re * re + im * im - frame
            back.append(mul_left(left_ref[parity], jnp.concatenate([weight * re, weight * im], axis=0)))
        top, bottom = back[0] + back[1], back[0] - back[1]
        re = jnp.concatenate([top[:half], bottom[:half]], axis=0)
        im = jnp.concatenate([top[half:], bottom[half:]], axis=0)
        even = mul_right(jnp.concatenate([re[:, :half], im[:, :half]], axis=1), right_ref[0])
        odd = mul_right(jnp.concatenate([re[:, half:], im[:, half:]], axis=1), right_ref[1])
        low, high = even + odd, even - odd
        re = jnp.concatenate([low[:, :half], high[:, :half]], axis=1)
        im = jnp.concatenate([low[:, half:], high[:, half:]], axis=1)
        p_re, p_im = rolled_probe(probe_ref, a_y, a_x)
        grads = (p_re * re + p_im * im, p_re * im - p_im * re)
        rows, cols = masks(a_y, a_x, size)
        for part in range(2):
            for row in range(2):
                for col in range(2):
                    keep = jnp.logical_and(rows == (row == 0), cols == (col == 0))
                    where = window(grad_ref, part, ys[row], xs[col], size)
                    where[...] += jnp.where(keep, grads[part], 0.0)


def whole(shape):
    return pl.BlockSpec(shape, lambda i, *refs: (0,) * len(shape))


def run_forward(info, field, probe, right, left):
    count, size = info.shape[1], probe.shape[1]
    return pl.pallas_call(
        functools.partial(forward_kernel, field.shape[1] // size),
        out_shape=jax.ShapeDtypeStruct((count, 2, size, size), f32),
        grid_spec=pltpu.PrefetchScalarGridSpec(
            num_scalar_prefetch=1,
            grid=(count,),
            in_specs=[whole(field.shape), whole(probe.shape), whole(right.shape), whole(left.shape)],
            out_specs=pl.BlockSpec((1, 2, size, size), lambda i, *refs: (i, 0, 0, 0)),
        ),
        compiler_params=pltpu.CompilerParams(vmem_limit_bytes=40 << 20),
        cost_estimate=pl.CostEstimate(
            flops=count * 24 * size**3, bytes_accessed=4 * (field.size + count * 2 * size**2), transcendentals=0
        ),
        name="forward",
    )(info, field, probe, right, left)


def run_backward(info, first, far, frames, probe, right, left, perm, extent, grad):
    slots, size = frames[0].shape[:2]
    count = slots * len(frames)
    tables = [probe, right, left, perm] + ([] if grad is None else [grad])

    def frame_spec(chunk):
        return pl.BlockSpec(
            (1, size, size), lambda i, info: (jnp.clip(i - chunk * slots, 0, slots - 1), 0, 0)
        )

    return pl.pallas_call(
        functools.partial(backward_kernel, extent // size, len(frames), grad is not None),
        out_shape=jax.ShapeDtypeStruct((2, extent, extent), f32),
        grid_spec=pltpu.PrefetchScalarGridSpec(
            num_scalar_prefetch=1,
            grid=(count,),
            in_specs=[pl.BlockSpec((1, 2, size, size), lambda i, info: (first + i, 0, 0, 0))]
            + [frame_spec(chunk) for chunk in range(len(frames))]
            + [whole(table.shape) for table in tables],
            out_specs=whole((2, extent, extent)),
            scratch_shapes=[pltpu.VMEM((2, size, size // 2), f32), pltpu.VMEM((size, size), f32)],
        ),
        compiler_params=pltpu.CompilerParams(vmem_limit_bytes=40 << 20),
        cost_estimate=pl.CostEstimate(
            flops=count * 24 * size**3, bytes_accessed=4 * count * 3 * size**2, transcendentals=0
        ),
        name="backward",
    )(info[:, first : first + count], far, *frames, *tables)


def from_sides(low_part, high_part, axis):
    count = lax.axis_size(axis)
    forward = [(i, i + 1) for i in range(count - 1)]
    backward = [(target, source) for source, target in forward]
    return lax.ppermute(high_part, axis, forward), lax.ppermute(low_part, axis, backward)


def per_device(object_field, probe, frames, positions, helpers, task_counts):
    tile, size = object_field.shape[1], probe.shape[1]
    half = size // 2
    extent = tile + 2 * half
    kept = frames[0, 0]
    sources, slots = kept.shape[:2]
    me = lax.axis_index("gx")
    paired = sources & (sources - 1) == 0
    ids = list(range(sources))

    def target_of(d, i):
        return i ^ d if paired else (i + d) % sources

    def source_of(d, i):
        return i ^ d if paired else (i - d + sources) % sources

    far_steps, near_steps = ids[sources // 2 :], ids[1 : sources // 2]
    tail = far_steps[2:]
    groups = [[0] + far_steps[:2] + near_steps[:1]]
    for steps in (near_steps[1:], tail[:-1], tail[-1:]):
        groups += [steps[i : i + 2] for i in range(0, len(steps), 2)]
    order = [d for group in groups for d in group]

    def chunk_of(d, at):
        return lax.dynamic_index_in_dim(kept, target_of(d, at), axis=0, keepdims=False)

    leading = {d: chunk_of(d, me) for d in far_steps[:2]}
    leading, sided = lax.optimization_barrier((leading, object_field))
    before, after = from_sides(sided[:, :, :half], sided[:, :, tile - half :], "gx")
    late, before, after = lax.optimization_barrier((me, before, after))
    field = jnp.concatenate([before, object_field, after], axis=2)
    before, after = from_sides(field[:, :half], field[:, tile - half :], "gy")
    field = jnp.concatenate([before, field, after], axis=1)

    offsets = positions[0, 0]
    tasks = offsets.shape[0]
    task_ids = jnp.arange(tasks, dtype=jnp.int32)
    valid = task_ids < task_counts[0, 0]
    helper_cols = helpers[0, 0, :, 0]
    same = helper_cols[:, None] == helper_cols[None, :]
    ranks = jnp.sum(jnp.logical_and(same, task_ids[None, :] < task_ids[:, None]), axis=1)
    slot_of = helper_cols * slots + ranks
    kinds = jnp.concatenate(
        [source_of(d, me) * slots + jnp.arange(slots, dtype=jnp.int32) for d in order]
    )
    hit = jnp.logical_and(slot_of[None, :] == kinds[:, None], valid[None, :]).astype(jnp.int32)
    info = jnp.stack(
        [
            jnp.sum(hit * (offsets[None, :, 0] + half), axis=1),
            jnp.sum(hit * (offsets[None, :, 1] + half), axis=1),
            jnp.sum(hit, axis=1),
        ]
    ).astype(jnp.int32)

    right, right_t, left, left_t, perm = (jnp.asarray(t) for t in dft_tables(size))
    far = run_forward(info, field, probe, right, left)
    arrived = {}
    for d in order:
        at = me if d == 0 else late
        if d in tail:
            past = far_steps[far_steps.index(d) - 2]
            at, arrived[past] = lax.optimization_barrier((at, arrived[past]))
        chunk = leading[d] if d in leading else chunk_of(d, at)
        arrived[d] = chunk if d == 0 else lax.ppermute(chunk, "gx", [(i, target_of(d, i)) for i in ids])

    summed, first = None, 0
    for group in groups:
        summed = run_backward(
            info, first, far, [arrived[d] for d in group], probe, right_t, left_t, perm, extent, summed
        )
        first += len(group) * slots

    top, middle, bottom = slice(0, half), slice(half, tile - half), slice(tile - half, tile)
    inner = summed[:, half : half + tile]
    sent = (
        summed[:, :half], summed[:, tile + half :], inner[:, middle, :half], inner[:, middle, tile + half :]
    )
    sent = lax.optimization_barrier(sent)
    north, south = from_sides(sent[0], sent[1], "gy")
    west_mid, east_mid = from_sides(sent[2], sent[3], "gx")
    north, south, west_mid, east_mid = lax.optimization_barrier((north, south, west_mid, east_mid))
    upper, lower = inner[:, top] + north, inner[:, bottom] + south
    ends = jnp.concatenate([upper, lower], axis=1)
    west_ends, east_ends = from_sides(ends[:, :, :half], ends[:, :, tile + half :], "gx")
    west = jnp.concatenate([west_ends[:, :half], west_mid, west_ends[:, half:]], axis=1)
    east = jnp.concatenate([east_ends[:, :half], east_mid, east_ends[:, half:]], axis=1)
    own = slice(half, half + tile)
    gradient = jnp.concatenate([upper[:, :, own], inner[:, middle, own], lower[:, :, own]], axis=1)
    gradient = gradient.at[:, :, :half].add(west)
    gradient = gradient.at[:, :, tile - half :].add(east)
    return object_field - step_size * (gradient + ridge * object_field)


def solution(mesh):
    in_specs = (
        P(None, "gy", "gx"),
        P(),
        P("gy", "gx", None, None, None, None),
        P("gy", "gx", None, None),
        P("gy", "gx", None, None),
        P("gy", "gx"),
    )
    out_specs = P(None, "gy", "gx")
    return jax.shard_map(
        per_device, mesh=mesh, in_specs=in_specs, out_specs=out_specs, check_vma=False
    )
```
